256 devices in a mesh: layer: 4 (over y), latent: 64 (over x, z, core).
Axes of the slice: x: 4, y: 4, z: 8, core: 2. Of those that a mesh axis runs over, the one named last changes fastest.
Arguments:
- acts: bfloat16 [4, 128, 3584], P('layer', 'latent'), may hold values from -6 to 6
- enc_weight: bfloat16 [4, 3584, 8192], P('layer', None, 'latent'), may hold values from -0.09375 to 0.09375
- enc_bias: float32 [4, 8192], P('layer', 'latent'), may hold values from -3 to 3
- active: int32 [4, 128, 8192], P('layer', None, 'latent'), may hold values 0 or 1
- dec_weight: bfloat16 [4, 4, 8192, 3584], P('layer', None, 'latent'), may hold values from -0.0625 to 0.0625
- dec_bias: float32 [4, 3584], replicated, may hold values from -3 to 3
- targets: bfloat16 [4, 128, 3584], P('layer', 'latent'), may hold values from -6 to 6
Outputs:
- grad_enc: bfloat16 [4, 3584, 8192], P('layer', None, 'latent')
- grad_enc_bias: float32 [4, 8192], P('layer', 'latent')
- grad_dec: bfloat16 [4, 4, 8192, 3584], P('layer', None, 'latent')
- grad_dec_bias: float32 [4, 3584], P('layer')
The draws below stay inside these ranges and needn't reach their ends.
All inputs are finite; a program needn't handle non-finite values. No bound on the sum of `active` on one device may be relied on, other than what follows from the above.
Results may differ from the reference program's by a relative error of at most 0.0075.
Values may be sent and summed in bfloat16 or wider, within the bound.
No kernel may reach another device: no remote copies, remote signals or barrier semaphores. Data moves between devices by JAX's collectives and lax.ppermute only.
A program may use at most 128 MiB of HBM per device.

```python
import jax
import jax.numpy as jnp

D = 3584
F = 8192
L = 4
B = 128


def place_ends(result, stream_key, low, top_value):
    dims = result.shape
    spot = [jax.random.randint(jax.random.fold_in(stream_key, axis), (), 0, dims[axis]) for axis in range(len(dims))]
    result = result.at[tuple(spot)].set(low)
    longest = dims.index(max(dims))
    spot[longest] = (spot[longest] + 1) % dims[longest]
    return result.at[tuple(spot)].set(top_value)


def level_of(stream_key, extent, pieces, low, high):
    level, own = 1.0, jax.random.fold_in(stream_key, 6)
    for dim, shards_of in pieces:
        heights = jnp.exp(jax.random.uniform(jax.random.fold_in(own, dim), (shards_of,), jnp.float32, low / len(pieces), high / len(pieces)))
        level = level * jnp.repeat(heights, extent[dim] // shards_of).reshape([-1 if axis == dim else 1 for axis in range(len(extent))])
    return level


def bell_draw(stream_key, shape, spread, bound, split=(), held_as=jnp.bfloat16):
    level = level_of(stream_key, shape, split, -0.22, 0.18) if split else 1.0
    values = jax.random.normal(stream_key, shape, jnp.float32) * spread * level
    return jnp.minimum(jnp.maximum(values, -bound), bound).astype(held_as)


def setup_inputs(seed: int = 0) -> dict:
    arg_keys = jax.random.split(jax.random.key(seed), 8)
    return {
        "acts": bell_draw(arg_keys[0], (L, B, D), 1.0, 6.0, ((0, 4), (1, 64))),
        "enc_weight": bell_draw(arg_keys[1], (L, D, F), D ** -0.5, 0.09375, ((0, 4), (2, 64))),
        "enc_bias": bell_draw(arg_keys[2], (L, F), 0.5, 3.0, ((0, 4), (1, 64)), jnp.float32),
        "active": place_ends((jax.random.randint(arg_keys[3], (L, B, F), 0, 4) < 1).astype(jnp.int32), jax.random.fold_in(arg_keys[3], 1), 0, 1),
        "dec_weight": bell_draw(arg_keys[4], (L, L, F, D), F ** -0.5, 0.0625, ((0, 4), (2, 64))),
        "dec_bias": bell_draw(arg_keys[5], (L, D), 0.5, 3.0, (), jnp.float32),
        "targets": bell_draw(arg_keys[6], (L, B, D), 1.0, 6.0, ((0, 4), (1, 64))),
    }


def reference(acts, enc_weight, enc_bias, active, dec_weight, dec_bias, targets):
    pre = jnp.einsum('lbd,ldf->lbf', acts.astype(jnp.float32), enc_weight.astype(jnp.float32)) + enc_bias[:, None, :]
    gate = active.astype(jnp.float32)
    feats = (pre * gate).astype(jnp.bfloat16)
    scale = B ** -0.5
    errors = []
    for target in range(L):
        total = jnp.zeros((B, D), jnp.float32)
        for source in range(target + 1):
            total = total + jnp.dot(feats[source], dec_weight[source, target], preferred_element_type=jnp.float32)
        total = total + dec_bias[target][None, :]
        errors.append(((total - targets[target].astype(jnp.float32)) * scale).astype(jnp.bfloat16))
    grad_rows = []
    enc_grads = []
    enc_bias_grads = []
    for source in range(L):
        back = jnp.zeros((B, F), jnp.float32)
        blocks = []
        for target in range(L):
            if target >= source:
                back = back + jnp.dot(errors[target], dec_weight[source, target].T, preferred_element_type=jnp.float32)
                blocks.append(jnp.dot(feats[source].T, errors[target], preferred_element_type=jnp.float32).astype(jnp.bfloat16))
            else:
                blocks.append(jnp.zeros((F, D), jnp.bfloat16))
        grad_rows.append(jnp.stack(blocks))
        dpre = (back * gate[source]).astype(jnp.bfloat16)
        enc_grads.append(jnp.dot(acts[source].T, dpre, preferred_element_type=jnp.float32).astype(jnp.bfloat16))
        enc_bias_grads.append(jnp.sum(dpre.astype(jnp.float32), axis=0))
    grad_dec_bias = jnp.stack([jnp.sum(e.astype(jnp.float32), axis=0) for e in errors])
    return jnp.stack(enc_grads), jnp.stack(enc_bias_grads), jnp.stack(grad_rows), grad_dec_bias
```

```python
import jax
import jax.numpy as jnp
from jax import lax
from jax.experimental import pallas as pl
from jax.experimental.pallas import tpu as pltpu
from jax.sharding import Mesh
from jax.sharding import PartitionSpec as P

LAYERS = 4
SWAP = [(0, 1), (1, 0)]
BF16 = jnp.bfloat16
F32 = jnp.float32


def ring(shift):
    return [(i, (i + shift) % LAYERS) for i in range(LAYERS)]


def grads_kernel(places, feats_t, own, other, decoder, back_in, *refs):
    grad_ref, back_ref = refs[-2:]
    step = pl.program_id(0)

    @pl.when(step == 0)
    def _():
        back_ref[...] = back_in[...]

    @pl.when(places[2] == 0)
    def _():
        grad_ref[...] = jnp.zeros_like(grad_ref)

    def work(block):
        tile = block[:, 0].reshape(feats_t.shape[1], block.shape[3])
        grad_ref[0] = jnp.dot(feats_t[...], tile, preferred_element_type=F32).astype(BF16)
        back_ref[...] += lax.dot_general(
            tile, decoder[0], (((1,), (1,)), ((), ())), preferred_element_type=F32
        )

    @pl.when((places[2] == 1) & (step < 2))
    def _():
        work(own)

    @pl.when((places[2] == 1) & (step >= 2))
    def _():
        work(other)


def grads_of_target(places, feats_t, own, other, decoder, back, grads):
    layers, latents, width = decoder.shape
    rows = feats_t.shape[1]
    quarter = width // 4

    def lanes(step, places):
        half = jnp.where(step < 2, places[1], 1 - places[1])
        return 2 * half + step % 2

    whole = lambda step, places: (0, 0)
    wide = lambda step, places: (places[0], 0, lanes(step, places))
    in_specs = [
        pl.BlockSpec((latents, rows), whole),
        pl.BlockSpec((rows // 8, 1, 8, quarter), lambda step, places: (0, jnp.minimum(step, 1), 0, 0)),
        pl.BlockSpec((rows // 8, 1, 8, quarter), lambda step, places: (0, jnp.maximum(step - 2, 0), 0, 0)),
        pl.BlockSpec((1, latents, quarter), wide),
        pl.BlockSpec((rows, latents), whole),
    ]
    operands = [places, feats_t, own, other, decoder, back]
    aliases = {}
    if grads is not None:
        in_specs.append(pl.BlockSpec(memory_space=pl.ANY))
        operands.append(grads)
        aliases = {6: 0}
    return pl.pallas_call(
        grads_kernel,
        grid_spec=pltpu.PrefetchScalarGridSpec(
            num_scalar_prefetch=1,
            grid=(4,),
            in_specs=in_specs,
            out_specs=[pl.BlockSpec((1, latents, quarter), wide), pl.BlockSpec((rows, latents), whole)],
        ),
        out_shape=[
            jax.ShapeDtypeStruct(decoder.shape, BF16),
            jax.ShapeDtypeStruct((rows, latents), F32),
        ],
        input_output_aliases=aliases,
        compiler_params=pltpu.CompilerParams(vmem_limit_bytes=32 * 1024 * 1024),
        cost_estimate=pl.CostEstimate(
            flops=4 * rows * latents * width, bytes_accessed=6 * latents * width, transcendentals=0
        ),
        name="grads_of_target",
    )(*operands)


def encoder_kernel(acts, back, gate, grad_ref, bias_ref):
    dpre = (back[...] * gate[...].astype(F32)).astype(BF16)
    grad_ref[...] = lax.dot_general(
        acts[...], dpre, (((0,), (0,)), ((), ())), preferred_element_type=F32
    ).astype(BF16)
    bias_ref[...] = jnp.sum(dpre.astype(F32), axis=0, keepdims=True)


def encoder_grads(acts, back, active):
    rows, width = acts.shape
    latents = back.shape[1]
    block = width // 7
    whole = lambda step: (0, 0)
    return pl.pallas_call(
        encoder_kernel,
        grid=(7,),
        in_specs=[
            pl.BlockSpec((rows, block), lambda step: (0, step)),
            pl.BlockSpec((rows, latents), whole),
            pl.BlockSpec((rows, latents), whole),
        ],
        out_specs=[pl.BlockSpec((block, latents), lambda step: (step, 0)), pl.BlockSpec((1, latents), whole)],
        out_shape=[jax.ShapeDtypeStruct((width, latents), BF16), jax.ShapeDtypeStruct((1, latents), F32)],
        compiler_params=pltpu.CompilerParams(vmem_limit_bytes=32 * 1024 * 1024),
        cost_estimate=pl.CostEstimate(
            flops=2 * rows * latents * width, bytes_accessed=4 * latents * width, transcendentals=0
        ),
        name="encoder_grads",
    )(acts, back, active)


def per_device(acts, enc_weight, enc_bias, active, dec_weight, dec_bias, targets):
    layer, core = lax.axis_index("y"), lax.axis_index("c")
    chip = lax.axis_index(("x", "z"))
    decoder = dec_weight[0]
    layers, latents, width = decoder.shape
    half, quarter = width // 2, width // 4
    rows = active.shape[1]
    scale = rows ** (-0.5)

    mine = lax.dynamic_slice_in_dim(decoder, core * half, half, axis=2)
    give = lax.dynamic_slice_in_dim(decoder, (1 - core) * half, half, axis=2)
    got = lax.ppermute(give, "c", SWAP)
    target_mine = lax.dynamic_slice_in_dim(targets[0], core * half, half, axis=1)
    target_give = lax.dynamic_slice_in_dim(targets[0], (1 - core) * half, half, axis=1)
    target_got = lax.ppermute(target_give, "c", SWAP)
    target_rows = jnp.where(
        core == 0,
        jnp.concatenate([target_mine, target_got], axis=0),
        jnp.concatenate([target_got, target_mine], axis=0),
    ).astype(F32)

    devices = rows // acts.shape[1]
    copies = jnp.broadcast_to(acts[0][None], (devices,) + acts.shape[1:])
    whole = lax.all_to_all(copies, ("x", "z", "c"), 0, 0, tiled=True).reshape(rows, width)
    pre = jnp.dot(whole, enc_weight[0], preferred_element_type=F32) + enc_bias[0][None, :]
    gate = active[0].astype(F32)
    feats = (pre * gate).astype(BF16)
    feats_other = lax.ppermute(feats, "c", SWAP)

    def partial(shift):
        target = (layer + shift) % layers
        first = lax.dynamic_index_in_dim(mine, target, 0, keepdims=False)
        second = lax.dynamic_index_in_dim(got, target, 0, keepdims=False)
        return jnp.dot(feats, first, preferred_element_type=F32) + jnp.dot(
            feats_other, second, preferred_element_type=F32
        )

    arrived = []
    for shift in (3, 2, 1):
        arrived.append(lax.ppermute(partial(shift).astype(BF16), "y", ring(shift)))
    total = partial(0)
    placed = lax.dynamic_update_slice_in_dim(
        jnp.zeros((rows, half), F32), target_rows, chip * target_rows.shape[0], 0
    )
    total = total - placed
    for shift, block in zip((3, 2, 1), arrived):
        total = total + jnp.where(layer >= shift, block.astype(F32), 0.0)
    chunks = (
        total.astype(BF16).reshape(rows // 8, 8, 2, quarter).transpose(0, 2, 1, 3).reshape(-1, 8, quarter)
    )
    pieces = lax.all_to_all(chunks, ("x", "z"), 0, 0, tiled=True)
    summed = jnp.sum(pieces.astype(F32), axis=0)
    bias = lax.dynamic_slice(dec_bias, (layer, core * half + (chip % 2) * quarter), (1, quarter))
    err = ((summed + bias) * scale).astype(BF16)
    err_copies = jnp.broadcast_to(err[None], (rows // 4, 8, quarter))
    own = lax.all_to_all(err_copies, ("x", "z"), 0, 0, tiled=True).reshape(rows // 8, 2, 8, quarter)

    errs = [own] + [lax.ppermute(own, "y", ring(-shift)) for shift in (1, 2, 3)]
    feats_t = feats.T
    back = jnp.zeros((rows, latents), F32)
    grads = None
    for shift, mine_err in enumerate(errs):
        other_err = lax.ppermute(mine_err, "c", SWAP)
        if shift == 0:
            sums = jnp.stack(
                [jnp.sum(e.astype(F32), axis=(0, 2)).reshape(half) for e in (mine_err, other_err)]
            )
            sums = jnp.where(core == 0, sums, sums[::-1]).reshape(1, width)
        places = jnp.stack(
            [(layer + shift) % layers, core, (layer + shift < layers).astype(jnp.int32)]
        ).astype(jnp.int32)
        grads, back = grads_of_target(places, feats_t, mine_err, other_err, decoder, back, grads)
    grad_enc, grad_enc_bias = encoder_grads(whole, back, active[0])
    return grad_enc[None], grad_enc_bias, grads[None], sums


def solution(mesh):
    split = Mesh(mesh.devices.reshape(4, 4, 8, 2), ("y", "x", "z", "c"))
    latent = ("x", "z", "c")
    return jax.shard_map(
        per_device,
        mesh=split,
        in_specs=(
            P("y", latent, None),
            P("y", None, latent),
            P("y", latent),
            P("y", None, latent),
            P("y", None, latent, None),
            P(),
            P("y", latent, None),
        ),
        out_specs=(
            P("y", None, latent),
            P("y", latent),
            P("y", None, latent, None),
            P("y", None),
        ),
        check_vma=False,
    )
```

```python
import jax
import jax.numpy as jnp
from jax import lax
from jax.experimental import pallas as pl
from jax.experimental.pallas import tpu as pltpu
from jax.sharding import Mesh
from jax.sharding import PartitionSpec as P

SWAP = [(0, 1), (1, 0)]
BF16 = jnp.bfloat16
F32 = jnp.float32
PARAMS = pltpu.CompilerParams(vmem_limit_bytes=8 * 1024 * 1024)


def whole_block(*shape):
    return pl.BlockSpec(shape, lambda step, places: (0,) * len(shape))


def cost(flops, moved):
    return pl.CostEstimate(flops=flops, bytes_accessed=moved, transcendentals=0)


def swap_halves(block):
    middle = block.shape[0] // 2
    return jnp.concatenate([block[middle:], block[:middle]], axis=0)


def recon_kernel(places, feats, feats_other, mine, got, placed, out):
    target = pl.program_id(0)

    @pl.when(target < places[0])
    def _():
        out[...] = jnp.zeros_like(out)

    @pl.when(target >= places[0])
    def _():
        total = jnp.dot(feats[...], mine[0], preferred_element_type=F32) + jnp.dot(
            feats_other[...], got[0], preferred_element_type=F32
        )
        out[0] = total.astype(BF16)

        @pl.when(target == places[0])
        def _():
            out[0] = (total - placed[...].astype(F32)).astype(BF16)


def recon_partials(places, feats, feats_other, mine, got, placed):
    layers, latents, half = got.shape
    rows = feats.shape[0]
    return pl.pallas_call(
        recon_kernel,
        grid_spec=pltpu.PrefetchScalarGridSpec(
            num_scalar_prefetch=1,
            grid=(layers,),
            in_specs=[
                whole_block(rows, latents),
                whole_block(rows, latents),
                pl.BlockSpec((1, latents, half), lambda step, places: (step, 0, 0)),
                pl.BlockSpec((1, latents, half), lambda step, places: (step, 0, 0)),
                whole_block(rows, half),
            ],
            out_specs=pl.BlockSpec((1, rows, half), lambda step, places: (step, 0, 0)),
        ),
        out_shape=jax.ShapeDtypeStruct((layers, rows, half), BF16),
        compiler_params=PARAMS,
        cost_estimate=cost(4 * layers * rows * latents * half, 6 * layers * rows * half),
        name="recon_partials",
    )(places, feats, feats_other, mine, got, placed)


def add_kernel(pieces, out):
    total = jnp.sum(pieces[...].astype(F32), axis=0)
    quarter = out.shape[2]
    for group in range(total.shape[0] // 8):
        for side in range(2):
            tile = total[8 * group : 8 * group + 8, side * quarter : (side + 1) * quarter]
            out[2 * group + side] = tile.astype(BF16)


def add_pieces(pieces):
    count, rows, half = pieces.shape
    quarter = half // 2
    return pl.pallas_call(
        add_kernel,
        grid=(rows // 16,),
        in_specs=[pl.BlockSpec((count, 16, half), lambda step: (0, step, 0))],
        out_specs=pl.BlockSpec((4, 8, quarter), lambda step: (step, 0, 0)),
        out_shape=jax.ShapeDtypeStruct((rows // 4, 8, quarter), BF16),
        compiler_params=PARAMS,
        cost_estimate=cost(count * rows * half, 2 * count * rows * half),
        name="add_pieces",
    )(pieces)


def grads_kernel(places, feats_t, errs, decoder, *refs):
    grad_ref, back_ref, sums_ref = refs[-3:]
    target = pl.program_id(0)
    quarter = errs.shape[4]
    rows = feats_t.shape[1]

    @pl.when(target == 0)
    def _():
        back_ref[...] = jnp.zeros_like(back_ref)

    @pl.when(target < places[0])
    def _():
        grad_ref[...] = jnp.zeros_like(grad_ref)

    @pl.when(target >= places[0])
    def _():
        for side in range(2):
            lanes = slice(side * quarter, (side + 1) * quarter)
            tile = errs[0, :, side].reshape(rows, quarter)
            grad_ref[0, :, lanes] = jnp.dot(feats_t[...], tile, preferred_element_type=F32).astype(BF16)
            back_ref[...] += lax.dot_general(
                tile, decoder[0, :, lanes], (((1,), (1,)), ((), ())), preferred_element_type=F32
            )

            @pl.when(target == places[0])
            def _():
                sums_ref[:, lanes] = jnp.sum(tile.astype(F32), axis=0, keepdims=True)


def grads_of_half(places, feats_t, errs, decoder, carried):
    layers, latents, half = decoder.shape
    rows = feats_t.shape[1]
    width = 2 * half
    wide = pl.BlockSpec((1, latents, half), lambda step, places: (step, 0, places[1]))
    in_specs = [
        whole_block(latents, rows),
        pl.BlockSpec((1,) + errs.shape[1:], lambda step, places: (step, 0, 0, 0, 0)),
        pl.BlockSpec((1, latents, half), lambda step, places: (step, 0, 0)),
    ]
    operands = [places, feats_t, errs, decoder]
    aliases = {}
    if carried is not None:
        in_specs += [pl.BlockSpec(memory_space=pl.ANY)] * 2
        operands += list(carried)
        aliases = {4: 0, 5: 2}
    return pl.pallas_call(
        grads_kernel,
        grid_spec=pltpu.PrefetchScalarGridSpec(
            num_scalar_prefetch=1,
            grid=(layers,),
            in_specs=in_specs,
            out_specs=[
                wide,
                whole_block(rows, latents),
                pl.BlockSpec((1, half), lambda step, places: (0, places[1])),
            ],
        ),
        out_shape=[
            jax.ShapeDtypeStruct((layers, latents, width), BF16),
            jax.ShapeDtypeStruct((rows, latents), F32),
            jax.ShapeDtypeStruct((1, width), F32),
        ],
        input_output_aliases=aliases,
        compiler_params=PARAMS,
        cost_estimate=cost(4 * layers * rows * latents * half, 6 * layers * latents * half),
        name="grads_of_half",
    )(*operands)


def encoder_kernel(same, apart, back, back_other, gate, grad_ref, bias_ref):
    dpre = ((back[...] + swap_halves(back_other[...])) * gate[...].astype(F32)).astype(BF16)
    middle = same.shape[0]
    over_rows = (((0,), (0,)), ((), ()))
    grad = lax.dot_general(same[...], dpre[:middle], over_rows, preferred_element_type=F32)
    grad += lax.dot_general(apart[...], dpre[middle:], over_rows, preferred_element_type=F32)
    grad_ref[...] = grad.astype(BF16)
    bias_ref[...] = jnp.sum(dpre.astype(F32), axis=0, keepdims=True)


def encoder_grads(same, apart, back, back_other, active):
    middle, width = same.shape
    rows, latents = back.shape
    block = width // 2
    whole = pl.BlockSpec((rows, latents), lambda step: (0, 0))
    flat = pl.BlockSpec((middle, block), lambda step: (0, step))
    return pl.pallas_call(
        encoder_kernel,
        grid=(2,),
        in_specs=[flat, flat, whole, whole, whole],
        out_specs=[
            pl.BlockSpec((block, latents), lambda step: (step, 0)),
            pl.BlockSpec((1, latents), lambda step: (0, 0)),
        ],
        out_shape=[jax.ShapeDtypeStruct((width, latents), BF16), jax.ShapeDtypeStruct((1, latents), F32)],
        compiler_params=PARAMS,
        cost_estimate=cost(2 * rows * latents * width, 4 * latents * width),
        name="encoder_grads",
    )(same, apart, back, back_other, active)


def per_device(acts, enc_weight, enc_bias, active, dec_weight, dec_bias, targets):
    layer, core = lax.axis_index("y"), lax.axis_index("c")
    chip, place = lax.axis_index(("x", "z")), lax.axis_index("z")
    decoder = dec_weight[0]
    layers, latents, width = decoder.shape
    half, quarter = width // 2, width // 4
    rows = active.shape[1]
    held = acts.shape[1]
    chips = rows // (2 * held)
    scale = rows ** (-0.5)

    copies = jnp.broadcast_to(acts[0][None], (chips, held, width))
    same = lax.all_to_all(copies, ("x", "z"), 0, 0, tiled=True).reshape(chips * held, width)

    give = lax.dynamic_slice_in_dim(decoder, (1 - core) * half, half, axis=2)
    mine = lax.dynamic_slice_in_dim(decoder, core * half, half, axis=2)
    got = lax.ppermute(give, "c", SWAP)
    target_mine = lax.dynamic_slice_in_dim(targets[0], core * half, half, axis=1)
    target_give = lax.dynamic_slice_in_dim(targets[0], (1 - core) * half, half, axis=1)
    target_got = lax.ppermute(target_give, "c", SWAP)
    placed = jnp.zeros((rows, half), BF16)
    placed = lax.dynamic_update_slice_in_dim(placed, target_mine, chip * held, 0)
    placed = lax.dynamic_update_slice_in_dim(placed, target_got, rows // 2 + chip * held, 0)
    by_core = active[0].reshape(chips, 2, held, latents)
    active_rows = jnp.concatenate(
        [
            lax.dynamic_index_in_dim(by_core, which, 1, keepdims=False).reshape(rows // 2, latents)
            for which in (core, 1 - core)
        ],
        axis=0,
    )

    bias = lax.dynamic_slice(dec_bias, (layer, core * half + (place % 2) * quarter), (1, quarter))
    same, mine, bias, active_rows = lax.optimization_barrier((same, mine, bias, active_rows))
    apart = lax.ppermute(same, "c", SWAP)
    pre = jnp.concatenate(
        [jnp.dot(part, enc_weight[0], preferred_element_type=F32) for part in (same, apart)], axis=0
    )
    feats = ((pre + enc_bias[0][None, :]) * active_rows.astype(F32)).astype(BF16)
    feats_other = swap_halves(lax.ppermute(feats, "c", SWAP))

    places = jnp.stack([layer, core]).astype(jnp.int32)
    partials = recon_partials(places, feats, feats_other, mine, got, placed)
    pieces = lax.all_to_all(partials.reshape(16, rows // 4, half), ("y", "x"), 0, 0, tiled=True)
    chunks = lax.all_to_all(add_pieces(pieces), "z", 0, 0, tiled=True)
    summed = jnp.sum(chunks.astype(F32), axis=0)
    err = ((summed + bias) * scale).astype(BF16)
    near = lax.all_to_all(jnp.broadcast_to(err[None], chunks.shape), "z", 0, 0, tiled=True)
    far = lax.all_to_all(jnp.broadcast_to(near[None], (16,) + near.shape), ("y", "x"), 0, 0, tiled=True)
    errs = far.reshape(layers, rows // 8, 2, 8, quarter)
    errs_other = lax.ppermute(errs, "c", SWAP)

    feats_t, feats_t_other = feats.T, swap_halves(feats).T
    grads, back, sums = grads_of_half(places, feats_t, errs, mine, None)
    places_other = jnp.stack([layer, 1 - core]).astype(jnp.int32)
    grads, back_other, sums = grads_of_half(places_other, feats_t_other, errs_other, give, (grads, sums))
    grad_enc, grad_enc_bias = encoder_grads(same, apart, back, back_other, active_rows)
    return grad_enc[None], grad_enc_bias, grads[None], sums


def solution(mesh):
    split = Mesh(mesh.devices.reshape(4, 4, 8, 2), ("y", "x", "z", "c"))
    latent = ("x", "z", "c")
    return jax.shard_map(
        per_device,
        mesh=split,
        in_specs=(
            P("y", latent, None),
            P("y", None, latent),
            P("y", latent),
            P("y", None, latent),
            P("y", None, latent, None),
            P(),
            P("y", latent, None),
        ),
        out_specs=(
            P("y", None, latent),
            P("y", latent),
            P("y", None, latent, None),
            P("y", None),
        ),
        check_vma=False,
    )
```

```python
import jax
import jax.numpy as jnp
from jax import lax
from jax.experimental import pallas as pl
from jax.experimental.pallas import tpu as pltpu
from jax.sharding import Mesh
from jax.sharding import PartitionSpec as P

SWAP = [(0, 1), (1, 0)]
BF16 = jnp.bfloat16
F32 = jnp.float32
VMEM = pl.BlockSpec(memory_space=pltpu.VMEM)
SMEM = pl.BlockSpec(memory_space=pltpu.SMEM)
ANY = pl.BlockSpec(memory_space=pl.ANY)
OVER_ROWS = (((0,), (0,)), ((), ()))


def params(mebibytes):
    return pltpu.CompilerParams(vmem_limit_bytes=mebibytes * 1024 * 1024)


def cost(flops, moved):
    return pl.CostEstimate(flops=flops, bytes_accessed=moved, transcendentals=0)


def swap_halves(block):
    middle = block.shape[0] // 2
    return jnp.concatenate([block[middle:], block[:middle]], axis=0)


def start_all(source, held, sems):
    copies = [pltpu.make_async_copy(source.at[i], held.at[i], sems.at[i]) for i in range(held.shape[0])]
    for copy in copies:
        copy.start()
    return copies


def half_of(source, side, held):
    half = held.shape[2]
    return source.at[:, :, pl.ds(pl.multiple_of(side * half, half), half)]


def recon_kernel(layer, feats, feats_other, mine, got, placed, out, held, out_held, mine_sems, got_sems, out_sems):
    layers, rows, _ = out_held.shape
    latents = feats.shape[1]
    loads = []
    for target in range(layers):
        for which, (source, sems) in enumerate(((mine, mine_sems), (got, got_sems))):
            place = held.at[target, pl.ds(which * latents, latents)]
            loads.append(pltpu.make_async_copy(source.at[target], place, sems.at[target]))
            loads[-1].start()
    leaving = [pltpu.make_async_copy(out_held.at[t], out.at[t], out_sems.at[t]) for t in range(layers)]
    both = jnp.concatenate([feats[...], swap_halves(feats_other[...])], axis=1)
    for target in range(layers):
        loads[2 * target].wait()
        loads[2 * target + 1].wait()

        @pl.when(target < layer[0])
        def _():
            out_held[target] = jnp.zeros(out_held.shape[1:], BF16)

        @pl.when(target > layer[0])
        def _():
            out_held[target] = jnp.dot(both, held[target], preferred_element_type=F32).astype(BF16)

        @pl.when(target == layer[0])
        def _():
            total = jnp.dot(both, held[target], preferred_element_type=F32)
            out_held[target] = (total - placed[...].astype(F32)).astype(BF16)

        leaving[target].start()
    for copy in leaving:
        copy.wait()


def recon_partials(layer, feats, feats_other, mine, got, placed):
    layers, latents, half = got.shape
    rows = feats.shape[0]
    sems = pltpu.SemaphoreType.DMA((layers,))
    return pl.pallas_call(
        recon_kernel,
        in_specs=[SMEM, VMEM, VMEM, ANY, ANY, VMEM],
        out_specs=ANY,
        out_shape=jax.ShapeDtypeStruct((layers, rows, half), BF16),
        scratch_shapes=[
            pltpu.VMEM((layers, 2 * latents, half), BF16),
            pltpu.VMEM((layers, rows, half), BF16),
            sems,
            sems,
            sems,
        ],
        compiler_params=params(14),
        cost_estimate=cost(4 * layers * rows * latents * half, 6 * layers * rows * half),
        name="recon_partials",
    )(layer, feats, feats_other, mine, got, placed)


def add_kernel(pieces, out):
    total = jnp.sum(pieces[...].astype(F32), axis=0)
    quarter = out.shape[2]
    for group in range(total.shape[0] // 8):
        for side in range(2):
            tile = total[8 * group : 8 * group + 8, side * quarter : (side + 1) * quarter]
            out[2 * group + side] = tile.astype(BF16)


def add_pieces(pieces):
    count, rows, half = pieces.shape
    quarter = half // 2
    return pl.pallas_call(
        add_kernel,
        grid=(rows // 16,),
        in_specs=[pl.BlockSpec((count, 16, half), lambda step: (0, step, 0))],
        out_specs=pl.BlockSpec((4, 8, quarter), lambda step: (step, 0, 0)),
        out_shape=jax.ShapeDtypeStruct((rows // 4, 8, quarter), BF16),
        compiler_params=params(8),
        cost_estimate=cost(count * rows * half, 2 * count * rows * half),
        name="add_pieces",
    )(pieces)


def half_of_targets(layer, side, feats, err_of, decoder_of, grads, held, sems, total, sums):
    layers, latents, half = held.shape
    quarter = half // 2
    rows = feats.shape[0]
    lanes = pl.ds(pl.multiple_of(side * half, half), half)
    leaving = [pltpu.make_async_copy(held.at[t], grads.at[t, :, lanes], sems.at[t]) for t in range(layers)]

    def tile(target, part):
        return err_of(target)[:, part].reshape(rows, quarter)

    for target in range(layers):
        err_of(target, wait=True)

        @pl.when(target < layer)
        def _():
            held[target] = jnp.zeros(held.shape[1:], BF16)

        @pl.when(target >= layer)
        def _():
            for part in range(2):
                held[target, :, part * quarter : (part + 1) * quarter] = lax.dot_general(
                    feats, tile(target, part), OVER_ROWS, preferred_element_type=F32
                ).astype(BF16)

        leaving[target].start()
    total[...] = jnp.zeros_like(total)
    for target in range(layers):
        decoder_of(target, wait=True)

        @pl.when(target >= layer)
        def _():
            for part in range(2):
                total[...] += lax.dot_general(
                    tile(target, part),
                    decoder_of(target)[:, part * quarter : (part + 1) * quarter],
                    (((1,), (1,)), ((), ())),
                    preferred_element_type=F32,
                )

        @pl.when(target == layer)
        def _():
            for part in range(2):
                sums[:, part * quarter : (part + 1) * quarter] = jnp.sum(
                    tile(target, part).astype(F32), axis=0, keepdims=True
                )

    return leaving


def own_half_kernel(places, feats, errs, decoder, grads, back, sums, decoder_held, held, decoder_sems, sems):
    loads = start_all(half_of(decoder, places[1], decoder_held), decoder_held, decoder_sems)

    def decoder_of(target, wait=False):
        if wait:
            loads[target].wait()
        return decoder_held.at[target]

    def err_of(target, wait=False):
        return errs.at[target]

    leaving = half_of_targets(places[0], places[1], feats[...], err_of, decoder_of, grads, held, sems, back, sums)
    for copy in leaving:
        copy.wait()


def own_half(places, feats, errs, decoder):
    layers, latents, width = decoder.shape
    half = width // 2
    rows = feats.shape[0]
    block = pltpu.VMEM((layers, latents, half), BF16)
    sems = pltpu.SemaphoreType.DMA((layers,))
    return pl.pallas_call(
        own_half_kernel,
        in_specs=[SMEM, VMEM, VMEM, ANY],
        out_specs=[ANY, VMEM, VMEM],
        out_shape=[
            jax.ShapeDtypeStruct((layers, latents, 2 * half), BF16),
            jax.ShapeDtypeStruct((rows, latents), F32),
            jax.ShapeDtypeStruct((1, half), F32),
        ],
        scratch_shapes=[block, block, sems, sems],
        compiler_params=params(14),
        cost_estimate=cost(4 * layers * rows * latents * half, 6 * layers * latents * half),
        name="own_half",
    )(places, feats, errs, decoder)


def other_half_kernel(
    places, feats, gate, back, own_sums, errs, decoder, same, apart, grads_in,
    grads, sums, grad_enc, enc_sums,
    decoder_held, held, enc_held, total, other_sums, decoder_sems, sems, enc_sems,
):
    loads = start_all(half_of(decoder, 1 - places[1], decoder_held), decoder_held, decoder_sems)

    def err_of(target, wait=False):
        return errs.at[target]

    def decoder_of(target, wait=False):
        if wait:
            loads[target].wait()
        return decoder_held.at[target]

    leaving = half_of_targets(
        places[0], 1 - places[1], swap_halves(feats[...]), err_of, decoder_of, grads, held, sems, total, other_sums
    )
    dpre = ((back[...] + swap_halves(total[...])) * gate[...].astype(F32)).astype(BF16)
    enc_sums[...] = jnp.sum(dpre.astype(F32), axis=0, keepdims=True)
    parts, block, _ = enc_held.shape
    middle = same.shape[0]
    for part in range(parts):
        lanes = slice(part * block, (part + 1) * block)
        enc_held[part] = (
            lax.dot_general(same[:, lanes], dpre[:middle], OVER_ROWS, preferred_element_type=F32)
            + lax.dot_general(apart[:, lanes], dpre[middle:], OVER_ROWS, preferred_element_type=F32)
        ).astype(BF16)
        copy = pltpu.make_async_copy(enc_held.at[part], grad_enc.at[pl.ds(part * block, block)], enc_sems.at[part])
        copy.start()
        leaving.append(copy)
    half = own_sums.shape[1]

    @pl.when(places[1] == 0)
    def _():
        sums[:, :half] = own_sums[...]
        sums[:, half:] = other_sums[...]

    @pl.when(places[1] == 1)
    def _():
        sums[:, :half] = other_sums[...]
        sums[:, half:] = own_sums[...]

    for copy in leaving:
        copy.wait()


def other_half(places, feats, gate, back, own_sums, errs, decoder, same, apart, grads):
    layers, latents, width = decoder.shape
    rows, half = feats.shape[0], width // 2
    block = pltpu.VMEM((layers, latents, half), BF16)
    sems = pltpu.SemaphoreType.DMA((layers,))
    return pl.pallas_call(
        other_half_kernel,
        in_specs=[SMEM, VMEM, VMEM, VMEM, VMEM, VMEM, ANY, VMEM, VMEM, ANY],
        out_specs=[ANY, VMEM, ANY, VMEM],
        out_shape=[
            jax.ShapeDtypeStruct(grads.shape, BF16),
            jax.ShapeDtypeStruct((1, width), F32),
            jax.ShapeDtypeStruct((width, latents), BF16),
            jax.ShapeDtypeStruct((1, latents), F32),
        ],
        scratch_shapes=[
            block,
            block,
            pltpu.VMEM((4, width // 4, latents), BF16),
            pltpu.VMEM((rows, latents), F32),
            pltpu.VMEM((1, half), F32),
            sems,
            sems,
            sems,
        ],
        input_output_aliases={9: 0},
        compiler_params=params(20),
        cost_estimate=cost(6 * layers * rows * latents * half, 8 * layers * latents * half),
        name="other_half",
    )(places, feats, gate, back, own_sums, errs, decoder, same, apart, grads)


def per_device(acts, enc_weight, enc_bias, active, dec_weight, dec_bias, targets):
    layer, core = lax.axis_index("y"), lax.axis_index("c")
    chip, place = lax.axis_index(("x", "z")), lax.axis_index("z")
    decoder = dec_weight[0]
    layers, latents, width = decoder.shape
    half, quarter = width // 2, width // 4
    rows = active.shape[1]
    held = acts.shape[1]
    chips = rows // (2 * held)
    scale = rows ** (-0.5)

    copies = jnp.broadcast_to(acts[0][None], (chips, held, width))
    same = lax.all_to_all(copies, ("x", "z"), 0, 0, tiled=True).reshape(chips * held, width)

    give = lax.dynamic_slice_in_dim(decoder, (1 - core) * half, half, axis=2)
    mine = lax.dynamic_slice_in_dim(decoder, core * half, half, axis=2)
    got = lax.ppermute(give, "c", SWAP)
    target_mine = lax.dynamic_slice_in_dim(targets[0], core * half, half, axis=1)
    target_give = lax.dynamic_slice_in_dim(targets[0], (1 - core) * half, half, axis=1)
    target_got = lax.ppermute(target_give, "c", SWAP)
    placed = jnp.zeros((rows, half), BF16)
    placed = lax.dynamic_update_slice_in_dim(placed, target_mine, chip * held, 0)
    placed = lax.dynamic_update_slice_in_dim(placed, target_got, rows // 2 + chip * held, 0)
    by_core = active[0].reshape(chips, 2, held, latents)
    active_rows = jnp.concatenate(
        [
            lax.dynamic_index_in_dim(by_core, which, 1, keepdims=False).reshape(rows // 2, latents)
            for which in (core, 1 - core)
        ],
        axis=0,
    )

    bias = lax.dynamic_slice(dec_bias, (layer, core * half + (place % 2) * quarter), (1, quarter))[0]
    same, mine, bias, active_rows = lax.optimization_barrier((same, mine, bias, active_rows))
    apart = lax.ppermute(same, "c", SWAP)
    pre = jnp.concatenate(
        [jnp.dot(part, enc_weight[0], preferred_element_type=F32) for part in (same, apart)], axis=0
    )
    feats = ((pre + enc_bias[0][None, :]) * active_rows.astype(F32)).astype(BF16)
    feats_other = lax.ppermute(feats, "c", SWAP)

    places = jnp.stack([layer, core]).astype(jnp.int32)
    partials = recon_partials(places, feats, feats_other, mine, got, placed)
    pieces = lax.all_to_all(partials.reshape(16, rows // 4, half), ("y", "x"), 0, 0, tiled=True)
    chunks = lax.all_to_all(add_pieces(pieces), "z", 0, 0, tiled=True)
    summed = jnp.sum(chunks.astype(F32), axis=0)
    err = ((summed + bias) * scale).astype(BF16)
    near = lax.all_to_all(jnp.broadcast_to(err[None], chunks.shape), "z", 0, 0, tiled=True)
    far = lax.all_to_all(jnp.broadcast_to(near[None], (16,) + near.shape), ("y", "x"), 0, 0, tiled=True)
    errs = far.reshape(layers, rows // 8, 2, 8, quarter)
    errs_other = lax.ppermute(errs, "c", SWAP)

    grads, back, own_sums = own_half(places, feats, errs, decoder)
    grads, sums, grad_enc, grad_enc_bias = other_half(
        places, feats, active_rows, back, own_sums, errs_other, decoder, same, apart, grads
    )
    return grad_enc[None], grad_enc_bias, grads[None], sums


def solution(mesh):
    split = Mesh(mesh.devices.reshape(4, 4, 8, 2), ("y", "x", "z", "c"))
    latent = ("x", "z", "c")
    return jax.shard_map(
        per_device,
        mesh=split,
        in_specs=(
            P("y", latent, None),
            P("y", None, latent),
            P("y", latent),
            P("y", None, latent),
            P("y", None, latent, None),
            P(),
            P("y", latent, None),
        ),
        out_specs=(
            P("y", None, latent),
            P("y", latent),
            P("y", None, latent, None),
            P("y", None),
        ),
        check_vma=False,
    )
```

```python
import jax
import jax.numpy as jnp
from jax import lax
from jax.experimental import pallas as pl
from jax.experimental.pallas import tpu as pltpu
from jax.sharding import Mesh
from jax.sharding import PartitionSpec as P

SWAP = [(0, 1), (1, 0)]
BF16 = jnp.bfloat16
F32 = jnp.float32
VMEM = pl.BlockSpec(memory_space=pltpu.VMEM)
SMEM = pl.BlockSpec(memory_space=pltpu.SMEM)
ANY = pl.BlockSpec(memory_space=pl.ANY)
OVER_ROWS = (((0,), (0,)), ((), ()))


def params(mebibytes):
    return pltpu.CompilerParams(vmem_limit_bytes=mebibytes * 1024 * 1024)


def cost(flops, moved):
    return pl.CostEstimate(flops=flops, bytes_accessed=moved, transcendentals=0)


def swap_halves(block):
    middle = block.shape[0] // 2
    return jnp.concatenate([block[middle:], block[:middle]], axis=0)


def start_all(source, held, sems):
    copies = [pltpu.make_async_copy(source.at[i], held.at[i], sems.at[i]) for i in range(held.shape[0])]
    for copy in copies:
        copy.start()
    return copies


def half_of(source, side, held):
    half = held.shape[2]
    return source.at[:, :, pl.ds(pl.multiple_of(side * half, half), half)]


def recon_kernel(layer, feats, feats_other, mine, got, placed, out):
    theirs = swap_halves(feats_other[...])
    for target in range(out.shape[0]):

        @pl.when(target < layer[0])
        def _():
            out[target] = jnp.zeros(out.shape[1:], BF16)

        @pl.when(target >= layer[0])
        def _():
            total = jnp.dot(feats[...], mine[target], preferred_element_type=F32) + jnp.dot(
                theirs, got[target], preferred_element_type=F32
            )
            out[target] = total.astype(BF16)

            @pl.when(target == layer[0])
            def _():
                out[target] = (total - placed[...].astype(F32)).astype(BF16)


def recon_partials(layer, feats, feats_other, mine, got, placed):
    layers, latents, half = got.shape
    rows = feats.shape[0]
    return pl.pallas_call(
        recon_kernel,
        in_specs=[SMEM, VMEM, VMEM, VMEM, VMEM, VMEM],
        out_specs=VMEM,
        out_shape=jax.ShapeDtypeStruct((layers, rows, half), BF16),
        compiler_params=params(10),
        cost_estimate=cost(4 * layers * rows * latents * half, 6 * layers * rows * half),
        name="recon_partials",
    )(layer, feats, feats_other, mine, got, placed)


def add_kernel(pieces, out):
    total = jnp.sum(pieces[...].astype(F32), axis=0)
    quarter = out.shape[2]
    for group in range(total.shape[0] // 8):
        for side in range(2):
            tile = total[8 * group : 8 * group + 8, side * quarter : (side + 1) * quarter]
            out[2 * group + side] = tile.astype(BF16)


def add_pieces(pieces):
    count, rows, half = pieces.shape
    quarter = half // 2
    return pl.pallas_call(
        add_kernel,
        grid=(rows // 16,),
        in_specs=[pl.BlockSpec((count, 16, half), lambda step: (0, step, 0))],
        out_specs=pl.BlockSpec((4, 8, quarter), lambda step: (step, 0, 0)),
        out_shape=jax.ShapeDtypeStruct((rows // 4, 8, quarter), BF16),
        compiler_params=params(8),
        cost_estimate=cost(count * rows * half, 2 * count * rows * half),
        name="add_pieces",
    )(pieces)


def half_of_targets(layer, side, feats, err_of, decoder_of, grads, held, sems, total, sums):
    layers, latents, half = held.shape
    quarter = half // 2
    rows = feats.shape[0]
    lanes = pl.ds(pl.multiple_of(side * half, half), half)
    leaving = [pltpu.make_async_copy(held.at[t], grads.at[t, :, lanes], sems.at[t]) for t in range(layers)]

    def tile(target, part):
        return err_of(target)[:, part].reshape(rows, quarter)

    total[...] = jnp.zeros_like(total)
    for target in range(layers):
        decoder_of(target, wait=True)

        @pl.when(target < layer)
        def _():
            held[target] = jnp.zeros(held.shape[1:], BF16)

        @pl.when(target >= layer)
        def _():
            for part in range(2):
                lanes_of_part = slice(part * quarter, (part + 1) * quarter)
                block = tile(target, part)
                held[target, :, lanes_of_part] = lax.dot_general(
                    feats, block, OVER_ROWS, preferred_element_type=F32
                ).astype(BF16)
                total[...] += lax.dot_general(
                    block,
                    decoder_of(target)[:, lanes_of_part],
                    (((1,), (1,)), ((), ())),
                    preferred_element_type=F32,
                )

        leaving[target].start()

        @pl.when(target == layer)
        def _():
            for part in range(2):
                sums[:, part * quarter : (part + 1) * quarter] = jnp.sum(
                    tile(target, part).astype(F32), axis=0, keepdims=True
                )

    return leaving


def own_half_kernel(places, feats, errs, decoder, grads, back, sums, decoder_held, held, decoder_sems, sems):
    loads = start_all(half_of(decoder, places[1], decoder_held), decoder_held, decoder_sems)

    def decoder_of(target, wait=False):
        if wait:
            loads[target].wait()
        return decoder_held.at[target]

    def err_of(target, wait=False):
        return errs.at[target]

    leaving = half_of_targets(places[0], places[1], feats[...], err_of, decoder_of, grads, held, sems, back, sums)
    for copy in leaving:
        copy.wait()


def own_half(places, feats, errs, decoder):
    layers, latents, width = decoder.shape
    half = width // 2
    rows = feats.shape[0]
    block = pltpu.VMEM((layers, latents, half), BF16)
    sems = pltpu.SemaphoreType.DMA((layers,))
    return pl.pallas_call(
        own_half_kernel,
        in_specs=[SMEM, VMEM, VMEM, ANY],
        out_specs=[ANY, VMEM, VMEM],
        out_shape=[
            jax.ShapeDtypeStruct((layers, latents, 2 * half), BF16),
            jax.ShapeDtypeStruct((rows, latents), F32),
            jax.ShapeDtypeStruct((1, half), F32),
        ],
        scratch_shapes=[block, block, sems, sems],
        compiler_params=params(14),
        cost_estimate=cost(4 * layers * rows * latents * half, 6 * layers * latents * half),
        name="own_half",
    )(places, feats, errs, decoder)


def other_half_kernel(
    places, feats, gate, back, own_sums, errs, decoder, same, apart, grads_in,
    grads, sums, grad_enc, enc_sums,
    decoder_held, held, enc_held, total, other_sums, decoder_sems, sems, enc_sems,
):
    loads = start_all(half_of(decoder, 1 - places[1], decoder_held), decoder_held, decoder_sems)

    def err_of(target, wait=False):
        return errs.at[target]

    def decoder_of(target, wait=False):
        if wait:
            loads[target].wait()
        return decoder_held.at[target]

    leaving = half_of_targets(
        places[0], 1 - places[1], swap_halves(feats[...]), err_of, decoder_of, grads, held, sems, total, other_sums
    )
    dpre = ((back[...] + swap_halves(total[...])) * gate[...].astype(F32)).astype(BF16)
    enc_sums[...] = jnp.sum(dpre.astype(F32), axis=0, keepdims=True)
    parts, block, _ = enc_held.shape
    middle = same.shape[0]
    for part in range(parts):
        lanes = slice(part * block, (part + 1) * block)
        enc_held[part] = (
            lax.dot_general(same[:, lanes], dpre[:middle], OVER_ROWS, preferred_element_type=F32)
            + lax.dot_general(apart[:, lanes], dpre[middle:], OVER_ROWS, preferred_element_type=F32)
        ).astype(BF16)
        copy = pltpu.make_async_copy(enc_held.at[part], grad_enc.at[pl.ds(part * block, block)], enc_sems.at[part])
        copy.start()
        leaving.append(copy)
    half = own_sums.shape[1]

    @pl.when(places[1] == 0)
    def _():
        sums[:, :half] = own_sums[...]
        sums[:, half:] = other_sums[...]

    @pl.when(places[1] == 1)
    def _():
        sums[:, :half] = other_sums[...]
        sums[:, half:] = own_sums[...]

    for copy in leaving:
        copy.wait()


def other_half(places, feats, gate, back, own_sums, errs, decoder, same, apart, grads):
    layers, latents, width = decoder.shape
    rows, half = feats.shape[0], width // 2
    block = pltpu.VMEM((layers, latents, half), BF16)
    sems = pltpu.SemaphoreType.DMA((layers,))
    return pl.pallas_call(
        other_half_kernel,
        in_specs=[SMEM, VMEM, VMEM, VMEM, VMEM, VMEM, ANY, VMEM, VMEM, ANY],
        out_specs=[ANY, VMEM, ANY, VMEM],
        out_shape=[
            jax.ShapeDtypeStruct(grads.shape, BF16),
            jax.ShapeDtypeStruct((1, width), F32),
            jax.ShapeDtypeStruct((width, latents), BF16),
            jax.ShapeDtypeStruct((1, latents), F32),
        ],
        scratch_shapes=[
            block,
            block,
            pltpu.VMEM((4, width // 4, latents), BF16),
            pltpu.VMEM((rows, latents), F32),
            pltpu.VMEM((1, half), F32),
            sems,
            sems,
            sems,
        ],
        input_output_aliases={9: 0},
        compiler_params=params(20),
        cost_estimate=cost(6 * layers * rows * latents * half, 8 * layers * latents * half),
        name="other_half",
    )(places, feats, gate, back, own_sums, errs, decoder, same, apart, grads)


def per_device(acts, enc_weight, enc_bias, active, dec_weight, dec_bias, targets):
    layer, core = lax.axis_index("y"), lax.axis_index("c")
    chip, place = lax.axis_index(("x", "z")), lax.axis_index("z")
    decoder = dec_weight[0]
    layers, latents, width = decoder.shape
    half, quarter = width // 2, width // 4
    rows = active.shape[1]
    held = acts.shape[1]
    chips = rows // (2 * held)
    scale = rows ** (-0.5)

    tiles = width // 128
    packed = acts[0].reshape(held, tiles, 128).transpose(1, 0, 2).reshape(tiles * held, 128)
    copies = jnp.broadcast_to(packed[None], (chips,) + packed.shape)
    same = lax.all_to_all(copies, ("x", "z"), 0, 0, tiled=True)
    same = same.reshape(chips, tiles, held, 128).transpose(0, 2, 1, 3).reshape(chips * held, width)

    give = lax.dynamic_slice_in_dim(decoder, (1 - core) * half, half, axis=2)
    mine = lax.dynamic_slice_in_dim(decoder, core * half, half, axis=2)
    got = lax.ppermute(give, "c", SWAP)
    target_mine = lax.dynamic_slice_in_dim(targets[0], core * half, half, axis=1)
    target_give = lax.dynamic_slice_in_dim(targets[0], (1 - core) * half, half, axis=1)
    target_got = lax.ppermute(target_give, "c", SWAP)
    placed = jnp.zeros((rows, half), BF16)
    placed = lax.dynamic_update_slice_in_dim(placed, target_mine, chip * held, 0)
    placed = lax.dynamic_update_slice_in_dim(placed, target_got, rows // 2 + chip * held, 0)
    by_core = active[0].reshape(chips, 2, held, latents)
    active_rows = jnp.concatenate(
        [
            lax.dynamic_index_in_dim(by_core, which, 1, keepdims=False).reshape(rows // 2, latents)
            for which in (core, 1 - core)
        ],
        axis=0,
    )

    bias = lax.dynamic_slice(dec_bias, (layer, core * half + (place % 2) * quarter), (1, quarter))[0]
    same, mine, bias, active_rows = lax.optimization_barrier((same, mine, bias, active_rows))
    apart = lax.ppermute(same, "c", SWAP)
    pre = jnp.concatenate(
        [jnp.dot(part, enc_weight[0], preferred_element_type=F32) for part in (same, apart)], axis=0
    )
    feats = ((pre + enc_bias[0][None, :]) * active_rows.astype(F32)).astype(BF16)
    feats_other = lax.ppermute(feats, "c", SWAP)

    places = jnp.stack([layer, core]).astype(jnp.int32)
    partials = recon_partials(places, feats, feats_other, mine, got, placed)
    pieces = lax.all_to_all(partials.reshape(16, rows // 4, half), ("y", "x"), 0, 0, tiled=True)
    chunks = lax.all_to_all(add_pieces(pieces), "z", 0, 0, tiled=True)
    summed = jnp.sum(chunks.astype(F32), axis=0)
    err = ((summed + bias) * scale).astype(BF16)
    near = lax.all_to_all(jnp.broadcast_to(err[None], chunks.shape), "z", 0, 0, tiled=True)
    far = lax.all_to_all(jnp.broadcast_to(near[None], (16,) + near.shape), ("y", "x"), 0, 0, tiled=True)
    errs = far.reshape(layers, rows // 8, 2, 8, quarter)
    errs_other = lax.ppermute(errs, "c", SWAP)

    grads, back, own_sums = own_half(places, feats, errs, decoder)
    grads, sums, grad_enc, grad_enc_bias = other_half(
        places, feats, active_rows, back, own_sums, errs_other, decoder, same, apart, grads
    )
    return grad_enc[None], grad_enc_bias, grads[None], sums


def solution(mesh):
    split = Mesh(mesh.devices.reshape(4, 4, 8, 2), ("y", "x", "z", "c"))
    latent = ("x", "z", "c")
    return jax.shard_map(
        per_device,
        mesh=split,
        in_specs=(
            P("y", latent, None),
            P("y", None, latent),
            P("y", latent),
            P("y", None, latent),
            P("y", None, latent, None),
            P(),
            P("y", latent, None),
        ),
        out_specs=(
            P("y", None, latent),
            P("y", latent),
            P("y", None, latent, None),
            P("y", None),
        ),
        check_vma=False,
    )
```

```python
import jax
import jax.numpy as jnp
from jax import lax
from jax.experimental import pallas as pl
from jax.experimental.pallas import tpu as pltpu
from jax.sharding import Mesh
from jax.sharding import PartitionSpec as P

SWAP = [(0, 1), (1, 0)]
BF16 = jnp.bfloat16
F32 = jnp.float32
VMEM = pl.BlockSpec(memory_space=pltpu.VMEM)
SMEM = pl.BlockSpec(memory_space=pltpu.SMEM)
ANY = pl.BlockSpec(memory_space=pl.ANY)
OVER_ROWS = (((0,), (0,)), ((), ()))


def params(mebibytes):
    return pltpu.CompilerParams(vmem_limit_bytes=mebibytes * 1024 * 1024)


def cost(flops, moved):
    return pl.CostEstimate(flops=flops, bytes_accessed=moved, transcendentals=0)


def swap_halves(block):
    middle = block.shape[0] // 2
    return jnp.concatenate([block[middle:], block[:middle]], axis=0)


def start_all(source, held, sems):
    copies = [pltpu.make_async_copy(source.at[i], held.at[i], sems.at[i]) for i in range(held.shape[0])]
    for copy in copies:
        copy.start()
    return copies


def copies_kernel(acts, out):
    tiles = [acts[0, :, start : start + 128].astype(F32) for start in range(0, acts.shape[2], 128)]
    packed = jnp.concatenate(tiles, axis=0).astype(BF16)
    out[...] = jnp.broadcast_to(packed[None], out.shape)


def copies_of_rows(acts, chips):
    _, held, width = acts.shape
    return pl.pallas_call(
        copies_kernel,
        in_specs=[VMEM],
        out_specs=VMEM,
        out_shape=jax.ShapeDtypeStruct((chips, held * width // 128, 128), BF16),
        compiler_params=params(4),
        cost_estimate=cost(0, 2 * chips * held * width),
        name="copies_of_rows",
    )(acts)


def half_of(source, side, held):
    half = held.shape[2]
    return source.at[:, :, pl.ds(pl.multiple_of(side * half, half), half)]


def recon_kernel(layer, feats, feats_other, mine, got, placed, out):
    both = jnp.concatenate([feats[...], swap_halves(feats_other[...])], axis=1)
    for target in range(out.shape[0]):

        @pl.when(target < layer[0])
        def _():
            out[target] = jnp.zeros(out.shape[1:], BF16)

        @pl.when(target >= layer[0])
        def _():
            decoders = jnp.concatenate([mine[target], got[target]], axis=0)
            total = jnp.dot(both, decoders, preferred_element_type=F32)
            out[target] = total.astype(BF16)

            @pl.when(target == layer[0])
            def _():
                out[target] = (total - placed[...].astype(F32)).astype(BF16)


def recon_partials(layer, feats, feats_other, mine, got, placed):
    layers, latents, half = got.shape
    rows = feats.shape[0]
    return pl.pallas_call(
        recon_kernel,
        in_specs=[SMEM, VMEM, VMEM, VMEM, VMEM, VMEM],
        out_specs=VMEM,
        out_shape=jax.ShapeDtypeStruct((layers, rows, half), BF16),
        compiler_params=params(10),
        cost_estimate=cost(4 * layers * rows * latents * half, 6 * layers * rows * half),
        name="recon_partials",
    )(layer, feats, feats_other, mine, got, placed)


def add_kernel(pieces, out):
    total = jnp.sum(pieces[...].astype(F32), axis=0)
    quarter = out.shape[2]
    for group in range(total.shape[0] // 8):
        for side in range(2):
            tile = total[8 * group : 8 * group + 8, side * quarter : (side + 1) * quarter]
            out[2 * group + side] = tile.astype(BF16)


def add_pieces(pieces):
    count, rows, half = pieces.shape
    quarter = half // 2
    return pl.pallas_call(
        add_kernel,
        grid=(rows // 16,),
        in_specs=[pl.BlockSpec((count, 16, half), lambda step: (0, step, 0))],
        out_specs=pl.BlockSpec((4, 8, quarter), lambda step: (step, 0, 0)),
        out_shape=jax.ShapeDtypeStruct((rows // 4, 8, quarter), BF16),
        compiler_params=params(8),
        cost_estimate=cost(count * rows * half, 2 * count * rows * half),
        name="add_pieces",
    )(pieces)


def half_of_targets(layer, side, feats, err_of, decoder_of, grads, held, sems, total, sums):
    layers, latents, half = held.shape
    quarter = half // 2
    rows = feats.shape[0]
    lanes = pl.ds(pl.multiple_of(side * half, half), half)
    leaving = [pltpu.make_async_copy(held.at[t], grads.at[t, :, lanes], sems.at[t]) for t in range(layers)]

    def tile(target, part):
        return err_of(target)[:, part].reshape(rows, quarter)

    total[...] = jnp.zeros_like(total)
    for target in range(layers):
        decoder_of(target, wait=True)

        @pl.when(target < layer)
        def _():
            held[target] = jnp.zeros(held.shape[1:], BF16)

        @pl.when(target >= layer)
        def _():
            for part in range(2):
                lanes_of_part = slice(part * quarter, (part + 1) * quarter)
                block = tile(target, part)
                held[target, :, lanes_of_part] = lax.dot_general(
                    feats, block, OVER_ROWS, preferred_element_type=F32
                ).astype(BF16)
                total[...] += lax.dot_general(
                    block,
                    decoder_of(target)[:, lanes_of_part],
                    (((1,), (1,)), ((), ())),
                    preferred_element_type=F32,
                )

        leaving[target].start()

        @pl.when(target == layer)
        def _():
            for part in range(2):
                sums[:, part * quarter : (part + 1) * quarter] = jnp.sum(
                    tile(target, part).astype(F32), axis=0, keepdims=True
                )

    return leaving


def own_half_kernel(places, feats, errs, decoder, grads, back, sums, decoder_held, held, decoder_sems, sems):
    loads = start_all(half_of(decoder, places[1], decoder_held), decoder_held, decoder_sems)

    def decoder_of(target, wait=False):
        if wait:
            loads[target].wait()
        return decoder_held.at[target]

    def err_of(target, wait=False):
        return errs.at[target]

    leaving = half_of_targets(places[0], places[1], feats[...], err_of, decoder_of, grads, held, sems, back, sums)
    for copy in leaving:
        copy.wait()


def own_half(places, feats, errs, decoder):
    layers, latents, width = decoder.shape
    half = width // 2
    rows = feats.shape[0]
    block = pltpu.VMEM((layers, latents, half), BF16)
    sems = pltpu.SemaphoreType.DMA((layers,))
    return pl.pallas_call(
        own_half_kernel,
        in_specs=[SMEM, VMEM, VMEM, ANY],
        out_specs=[ANY, VMEM, VMEM],
        out_shape=[
            jax.ShapeDtypeStruct((layers, latents, 2 * half), BF16),
            jax.ShapeDtypeStruct((rows, latents), F32),
            jax.ShapeDtypeStruct((1, half), F32),
        ],
        scratch_shapes=[block, block, sems, sems],
        compiler_params=params(14),
        cost_estimate=cost(4 * layers * rows * latents * half, 6 * layers * latents * half),
        name="own_half",
    )(places, feats, errs, decoder)


def other_half_kernel(
    places, feats, gate, back, own_sums, errs, decoder, same, apart, grads_in,
    grads, sums, grad_enc, enc_sums,
    decoder_held, held, enc_held, total, other_sums, decoder_sems, sems, enc_sems,
):
    loads = start_all(half_of(decoder, 1 - places[1], decoder_held), decoder_held, decoder_sems)

    def err_of(target, wait=False):
        return errs.at[target]

    def decoder_of(target, wait=False):
        if wait:
            loads[target].wait()
        return decoder_held.at[target]

    leaving = half_of_targets(
        places[0], 1 - places[1], swap_halves(feats[...]), err_of, decoder_of, grads, held, sems, total, other_sums
    )
    dpre = ((back[...] + swap_halves(total[...])) * gate[...].astype(F32)).astype(BF16)
    enc_sums[...] = jnp.sum(dpre.astype(F32), axis=0, keepdims=True)
    parts, block, _ = enc_held.shape
    middle = same.shape[0]
    for part in range(parts):
        lanes = slice(part * block, (part + 1) * block)
        enc_held[part] = (
            lax.dot_general(same[:, lanes], dpre[:middle], OVER_ROWS, preferred_element_type=F32)
            + lax.dot_general(apart[:, lanes], dpre[middle:], OVER_ROWS, preferred_element_type=F32)
        ).astype(BF16)
        copy = pltpu.make_async_copy(enc_held.at[part], grad_enc.at[pl.ds(part * block, block)], enc_sems.at[part])
        copy.start()
        leaving.append(copy)
    half = own_sums.shape[1]

    @pl.when(places[1] == 0)
    def _():
        sums[:, :half] = own_sums[...]
        sums[:, half:] = other_sums[...]

    @pl.when(places[1] == 1)
    def _():
        sums[:, :half] = other_sums[...]
        sums[:, half:] = own_sums[...]

    for copy in leaving:
        copy.wait()


def other_half(places, feats, gate, back, own_sums, errs, decoder, same, apart, grads):
    layers, latents, width = decoder.shape
    rows, half = feats.shape[0], width // 2
    block = pltpu.VMEM((layers, latents, half), BF16)
    sems = pltpu.SemaphoreType.DMA((layers,))
    return pl.pallas_call(
        other_half_kernel,
        in_specs=[SMEM, VMEM, VMEM, VMEM, VMEM, VMEM, ANY, VMEM, VMEM, ANY],
        out_specs=[ANY, VMEM, ANY, VMEM],
        out_shape=[
            jax.ShapeDtypeStruct(grads.shape, BF16),
            jax.ShapeDtypeStruct((1, width), F32),
            jax.ShapeDtypeStruct((width, latents), BF16),
            jax.ShapeDtypeStruct((1, latents), F32),
        ],
        scratch_shapes=[
            block,
            block,
            pltpu.VMEM((4, width // 4, latents), BF16),
            pltpu.VMEM((rows, latents), F32),
            pltpu.VMEM((1, half), F32),
            sems,
            sems,
            sems,
        ],
        input_output_aliases={9: 0},
        compiler_params=params(20),
        cost_estimate=cost(6 * layers * rows * latents * half, 8 * layers * latents * half),
        name="other_half",
    )(places, feats, gate, back, own_sums, errs, decoder, same, apart, grads)


def per_device(acts, enc_weight, enc_bias, active, dec_weight, dec_bias, targets):
    layer, core = lax.axis_index("y"), lax.axis_index("c")
    chip, place = lax.axis_index(("x", "z")), lax.axis_index("z")
    decoder = dec_weight[0]
    layers, latents, width = decoder.shape
    half, quarter = width // 2, width // 4
    rows = active.shape[1]
    held = acts.shape[1]
    chips = rows // (2 * held)
    scale = rows ** (-0.5)

    tiles = width // 128
    copies = copies_of_rows(acts, chips)
    same = lax.all_to_all(copies, ("x", "z"), 0, 0, tiled=True)
    same = same.reshape(chips, tiles, held, 128).transpose(0, 2, 1, 3).reshape(chips * held, width)

    give = lax.dynamic_slice_in_dim(decoder, (1 - core) * half, half, axis=2)
    mine = lax.dynamic_slice_in_dim(decoder, core * half, half, axis=2)
    got = lax.ppermute(give, "c", SWAP)
    target_mine = lax.dynamic_slice_in_dim(targets[0], core * half, half, axis=1)
    target_give = lax.dynamic_slice_in_dim(targets[0], (1 - core) * half, half, axis=1)
    target_got = lax.ppermute(target_give, "c", SWAP)
    placed = jnp.zeros((rows, half), BF16)
    placed = lax.dynamic_update_slice_in_dim(placed, target_mine, chip * held, 0)
    placed = lax.dynamic_update_slice_in_dim(placed, target_got, rows // 2 + chip * held, 0)
    by_core = active[0].reshape(chips, 2, held, latents)
    active_rows = jnp.concatenate(
        [
            lax.dynamic_index_in_dim(by_core, which, 1, keepdims=False).reshape(rows // 2, latents)
            for which in (core, 1 - core)
        ],
        axis=0,
    )

    bias = lax.dynamic_slice(dec_bias, (layer, core * half + (place % 2) * quarter), (1, quarter))[0]
    same, mine, bias, active_rows = lax.optimization_barrier((same, mine, bias, active_rows))
    apart = lax.ppermute(same, "c", SWAP)
    pre = jnp.concatenate(
        [jnp.dot(part, enc_weight[0], preferred_element_type=F32) for part in (same, apart)], axis=0
    )
    feats = ((pre + enc_bias[0][None, :]) * active_rows.astype(F32)).astype(BF16)
    feats_other = lax.ppermute(feats, "c", SWAP)

    places = jnp.stack([layer, core]).astype(jnp.int32)
    partials = recon_partials(places, feats, feats_other, mine, got, placed)
    pieces = lax.all_to_all(partials.reshape(16, rows // 4, half), ("y", "x"), 0, 0, tiled=True)
    chunks = lax.all_to_all(add_pieces(pieces), "z", 0, 0, tiled=True)
    summed = jnp.sum(chunks.astype(F32), axis=0)
    err = ((summed + bias) * scale).astype(BF16)
    near = lax.all_to_all(jnp.broadcast_to(err[None], chunks.shape), "z", 0, 0, tiled=True)
    far = lax.all_to_all(jnp.broadcast_to(near[None], (16,) + near.shape), ("y", "x"), 0, 0, tiled=True)
    errs = far.reshape(layers, rows // 8, 2, 8, quarter)
    errs_other = lax.ppermute(errs, "c", SWAP)

    grads, back, own_sums = own_half(places, feats, errs, decoder)
    grads, sums, grad_enc, grad_enc_bias = other_half(
        places, feats, active_rows, back, own_sums, errs_other, decoder, same, apart, grads
    )
    return grad_enc[None], grad_enc_bias, grads[None], sums


def solution(mesh):
    split = Mesh(mesh.devices.reshape(4, 4, 8, 2), ("y", "x", "z", "c"))
    latent = ("x", "z", "c")
    return jax.shard_map(
        per_device,
        mesh=split,
        in_specs=(
            P("y", latent, None),
            P("y", None, latent),
            P("y", latent),
            P("y", None, latent),
            P("y", None, latent, None),
            P(),
            P("y", latent, None),
        ),
        out_specs=(
            P("y", None, latent),
            P("y", latent),
            P("y", None, latent, None),
            P("y", None),
        ),
        check_vma=False,
    )
```

```python
import jax
import jax.numpy as jnp
from jax import lax
from jax.experimental import pallas as pl
from jax.experimental.pallas import tpu as pltpu
from jax.sharding import Mesh
from jax.sharding import PartitionSpec as P

SWAP = [(0, 1), (1, 0)]
BF16 = jnp.bfloat16
F32 = jnp.float32
VMEM = pl.BlockSpec(memory_space=pltpu.VMEM)
SMEM = pl.BlockSpec(memory_space=pltpu.SMEM)
ANY = pl.BlockSpec(memory_space=pl.ANY)
OVER_ROWS = (((0,), (0,)), ((), ()))


def params(mebibytes):
    return pltpu.CompilerParams(vmem_limit_bytes=mebibytes * 1024 * 1024)


def cost(flops, moved):
    return pl.CostEstimate(flops=flops, bytes_accessed=moved, transcendentals=0)


def swap_halves(block):
    middle = block.shape[0] // 2
    return jnp.concatenate([block[middle:], block[:middle]], axis=0)


def start_all(source, held, sems):
    copies = [pltpu.make_async_copy(source.at[i], held.at[i], sems.at[i]) for i in range(held.shape[0])]
    for copy in copies:
        copy.start()
    return copies


def copies_kernel(acts, out):
    tiles = [acts[0, :, start : start + 128].astype(F32) for start in range(0, acts.shape[2], 128)]
    packed = jnp.concatenate(tiles, axis=0).astype(BF16)
    out[...] = jnp.broadcast_to(packed[None], out.shape)


def copies_of_rows(acts, chips):
    _, held, width = acts.shape
    return pl.pallas_call(
        copies_kernel,
        in_specs=[VMEM],
        out_specs=VMEM,
        out_shape=jax.ShapeDtypeStruct((chips, held * width // 128, 128), BF16),
        compiler_params=params(4),
        cost_estimate=cost(0, 2 * chips * held * width),
        name="copies_of_rows",
    )(acts)


def half_of(source, side, held):
    half = held.shape[2]
    return source.at[:, :, pl.ds(pl.multiple_of(side * half, half), half)]


def recon_kernel(layer, feats, feats_other, mine, got, placed, out):
    both = jnp.concatenate([feats[...], swap_halves(feats_other[...])], axis=1)
    for target in range(out.shape[0]):

        @pl.when(target < layer[0])
        def _():
            out[target] = jnp.zeros(out.shape[1:], BF16)

        @pl.when(target >= layer[0])
        def _():
            decoders = jnp.concatenate([mine[target], got[target]], axis=0)
            total = jnp.dot(both, decoders, preferred_element_type=F32)
            out[target] = total.astype(BF16)

            @pl.when(target == layer[0])
            def _():
                out[target] = (total - placed[...].astype(F32)).astype(BF16)


def recon_partials(layer, feats, feats_other, mine, got, placed):
    layers, latents, half = got.shape
    rows = feats.shape[0]
    return pl.pallas_call(
        recon_kernel,
        in_specs=[SMEM, VMEM, VMEM, VMEM, VMEM, VMEM],
        out_specs=VMEM,
        out_shape=jax.ShapeDtypeStruct((layers, rows, half), BF16),
        compiler_params=params(10),
        cost_estimate=cost(4 * layers * rows * latents * half, 6 * layers * rows * half),
        name="recon_partials",
    )(layer, feats, feats_other, mine, got, placed)


def add_kernel(pieces, out):
    total = jnp.sum(pieces[...].astype(F32), axis=0)
    quarter = out.shape[2]
    for group in range(total.shape[0] // 8):
        for side in range(2):
            tile = total[8 * group : 8 * group + 8, side * quarter : (side + 1) * quarter]
            out[2 * group + side] = tile.astype(BF16)


def add_pieces(pieces):
    count, rows, half = pieces.shape
    quarter = half // 2
    return pl.pallas_call(
        add_kernel,
        grid=(rows // 16,),
        in_specs=[pl.BlockSpec((count, 16, half), lambda step: (0, step, 0))],
        out_specs=pl.BlockSpec((4, 8, quarter), lambda step: (step, 0, 0)),
        out_shape=jax.ShapeDtypeStruct((rows // 4, 8, quarter), BF16),
        compiler_params=params(8),
        cost_estimate=cost(count * rows * half, 2 * count * rows * half),
        name="add_pieces",
    )(pieces)


def half_of_targets(layer, side, feats, err_of, decoder_of, grads, held, sems, total, sums):
    layers, latents, half = held.shape
    quarter = half // 2
    rows = feats.shape[0]
    lanes = pl.ds(pl.multiple_of(side * half, half), half)
    leaving = [pltpu.make_async_copy(held.at[t], grads.at[t, :, lanes], sems.at[t]) for t in range(layers)]

    def tile(target, part):
        return err_of(target)[:, part].reshape(rows, quarter)

    total[...] = jnp.zeros_like(total)
    for target in range(layers):
        decoder_of(target, wait=True)

        @pl.when(target < layer)
        def _():
            held[target] = jnp.zeros(held.shape[1:], BF16)

        @pl.when(target >= layer)
        def _():
            block = jnp.concatenate([tile(target, part) for part in range(2)], axis=1)
            held[target] = lax.dot_general(feats, block, OVER_ROWS, preferred_element_type=F32).astype(BF16)
            total[...] += lax.dot_general(
                block, decoder_of(target)[...], (((1,), (1,)), ((), ())), preferred_element_type=F32
            )

        leaving[target].start()

        @pl.when(target == layer)
        def _():
            for part in range(2):
                sums[:, part * quarter : (part + 1) * quarter] = jnp.sum(
                    tile(target, part).astype(F32), axis=0, keepdims=True
                )

    return leaving


def own_half_kernel(places, feats, errs, decoder, grads, back, sums, decoder_held, held, decoder_sems, sems):
    loads = start_all(half_of(decoder, places[1], decoder_held), decoder_held, decoder_sems)

    def decoder_of(target, wait=False):
        if wait:
            loads[target].wait()
        return decoder_held.at[target]

    def err_of(target, wait=False):
        return errs.at[target]

    leaving = half_of_targets(places[0], places[1], feats[...], err_of, decoder_of, grads, held, sems, back, sums)
    for copy in leaving:
        copy.wait()


def own_half(places, feats, errs, decoder):
    layers, latents, width = decoder.shape
    half = width // 2
    rows = feats.shape[0]
    block = pltpu.VMEM((layers, latents, half), BF16)
    sems = pltpu.SemaphoreType.DMA((layers,))
    return pl.pallas_call(
        own_half_kernel,
        in_specs=[SMEM, VMEM, VMEM, ANY],
        out_specs=[ANY, VMEM, VMEM],
        out_shape=[
            jax.ShapeDtypeStruct((layers, latents, 2 * half), BF16),
            jax.ShapeDtypeStruct((rows, latents), F32),
            jax.ShapeDtypeStruct((1, half), F32),
        ],
        scratch_shapes=[block, block, sems, sems],
        compiler_params=params(14),
        cost_estimate=cost(4 * layers * rows * latents * half, 6 * layers * latents * half),
        name="own_half",
    )(places, feats, errs, decoder)


def other_half_kernel(
    places, feats, gate, back, own_sums, errs, decoder, same, apart, grads_in,
    grads, sums, grad_enc, enc_sums,
    decoder_held, held, enc_held, total, other_sums, decoder_sems, sems, enc_sems,
):
    loads = start_all(half_of(decoder, 1 - places[1], decoder_held), decoder_held, decoder_sems)

    def err_of(target, wait=False):
        return errs.at[target]

    def decoder_of(target, wait=False):
        if wait:
            loads[target].wait()
        return decoder_held.at[target]

    leaving = half_of_targets(
        places[0], 1 - places[1], swap_halves(feats[...]), err_of, decoder_of, grads, held, sems, total, other_sums
    )
    dpre = ((back[...] + swap_halves(total[...])) * gate[...].astype(F32)).astype(BF16)
    enc_sums[...] = jnp.sum(dpre.astype(F32), axis=0, keepdims=True)
    parts, block, _ = enc_held.shape
    middle = same.shape[0]
    for part in range(parts):
        lanes = slice(part * block, (part + 1) * block)
        enc_held[part] = (
            lax.dot_general(same[:, lanes], dpre[:middle], OVER_ROWS, preferred_element_type=F32)
            + lax.dot_general(apart[:, lanes], dpre[middle:], OVER_ROWS, preferred_element_type=F32)
        ).astype(BF16)
        copy = pltpu.make_async_copy(enc_held.at[part], grad_enc.at[pl.ds(part * block, block)], enc_sems.at[part])
        copy.start()
        leaving.append(copy)
    half = own_sums.shape[1]

    @pl.when(places[1] == 0)
    def _():
        sums[:, :half] = own_sums[...]
        sums[:, half:] = other_sums[...]

    @pl.when(places[1] == 1)
    def _():
        sums[:, :half] = other_sums[...]
        sums[:, half:] = own_sums[...]

    for copy in leaving:
        copy.wait()


def other_half(places, feats, gate, back, own_sums, errs, decoder, same, apart, grads):
    layers, latents, width = decoder.shape
    rows, half = feats.shape[0], width // 2
    block = pltpu.VMEM((layers, latents, half), BF16)
    sems = pltpu.SemaphoreType.DMA((layers,))
    return pl.pallas_call(
        other_half_kernel,
        in_specs=[SMEM, VMEM, VMEM, VMEM, VMEM, VMEM, ANY, VMEM, VMEM, ANY],
        out_specs=[ANY, VMEM, ANY, VMEM],
        out_shape=[
            jax.ShapeDtypeStruct(grads.shape, BF16),
            jax.ShapeDtypeStruct((1, width), F32),
            jax.ShapeDtypeStruct((width, latents), BF16),
            jax.ShapeDtypeStruct((1, latents), F32),
        ],
        scratch_shapes=[
            block,
            block,
            pltpu.VMEM((4, width // 4, latents), BF16),
            pltpu.VMEM((rows, latents), F32),
            pltpu.VMEM((1, half), F32),
            sems,
            sems,
            sems,
        ],
        input_output_aliases={9: 0},
        compiler_params=params(20),
        cost_estimate=cost(6 * layers * rows * latents * half, 8 * layers * latents * half),
        name="other_half",
    )(places, feats, gate, back, own_sums, errs, decoder, same, apart, grads)


def per_device(acts, enc_weight, enc_bias, active, dec_weight, dec_bias, targets):
    layer, core = lax.axis_index("y"), lax.axis_index("c")
    chip, place = lax.axis_index(("x", "z")), lax.axis_index("z")
    decoder = dec_weight[0]
    layers, latents, width = decoder.shape
    half, quarter = width // 2, width // 4
    rows = active.shape[1]
    held = acts.shape[1]
    chips = rows // (2 * held)
    scale = rows ** (-0.5)

    tiles = width // 128
    copies = copies_of_rows(acts, chips)
    same = lax.all_to_all(copies, ("x", "z"), 0, 0, tiled=True)
    same = same.reshape(chips, tiles, held, 128).transpose(0, 2, 1, 3).reshape(chips * held, width)

    give = lax.dynamic_slice_in_dim(decoder, (1 - core) * half, half, axis=2)
    mine = lax.dynamic_slice_in_dim(decoder, core * half, half, axis=2)
    got = lax.ppermute(give, "c", SWAP)
    target_mine = lax.dynamic_slice_in_dim(targets[0], core * half, half, axis=1)
    target_give = lax.dynamic_slice_in_dim(targets[0], (1 - core) * half, half, axis=1)
    target_got = lax.ppermute(target_give, "c", SWAP)
    placed = jnp.zeros((rows, half), BF16)
    placed = lax.dynamic_update_slice_in_dim(placed, target_mine, chip * held, 0)
    placed = lax.dynamic_update_slice_in_dim(placed, target_got, rows // 2 + chip * held, 0)
    by_core = active[0].reshape(chips, 2, held, latents)
    active_rows = jnp.concatenate(
        [
            lax.dynamic_index_in_dim(by_core, which, 1, keepdims=False).reshape(rows // 2, latents)
            for which in (core, 1 - core)
        ],
        axis=0,
    )

    bias = lax.dynamic_slice(dec_bias, (layer, core * half + (place % 2) * quarter), (1, quarter))[0]
    same, mine, bias, active_rows = lax.optimization_barrier((same, mine, bias, active_rows))
    apart = lax.ppermute(same, "c", SWAP)
    pre = jnp.concatenate(
        [jnp.dot(part, enc_weight[0], preferred_element_type=F32) for part in (same, apart)], axis=0
    )
    feats = ((pre + enc_bias[0][None, :]) * active_rows.astype(F32)).astype(BF16)
    feats_other = lax.ppermute(feats, "c", SWAP)

    places = jnp.stack([layer, core]).astype(jnp.int32)
    partials = recon_partials(places, feats, feats_other, mine, got, placed)
    pieces = lax.all_to_all(partials.reshape(16, rows // 4, half), ("y", "x"), 0, 0, tiled=True)
    chunks = lax.all_to_all(add_pieces(pieces), "z", 0, 0, tiled=True)
    summed = jnp.sum(chunks.astype(F32), axis=0)
    err = ((summed + bias) * scale).astype(BF16)
    near = lax.all_to_all(jnp.broadcast_to(err[None], chunks.shape), "z", 0, 0, tiled=True)
    far = lax.all_to_all(jnp.broadcast_to(near[None], (16,) + near.shape), ("y", "x"), 0, 0, tiled=True)
    errs = far.reshape(layers, rows // 8, 2, 8, quarter)
    errs_other = lax.ppermute(errs, "c", SWAP)

    grads, back, own_sums = own_half(places, feats, errs, decoder)
    grads, sums, grad_enc, grad_enc_bias = other_half(
        places, feats, active_rows, back, own_sums, errs_other, decoder, same, apart, grads
    )
    return grad_enc[None], grad_enc_bias, grads[None], sums


def solution(mesh):
    split = Mesh(mesh.devices.reshape(4, 4, 8, 2), ("y", "x", "z", "c"))
    latent = ("x", "z", "c")
    return jax.shard_map(
        per_device,
        mesh=split,
        in_specs=(
            P("y", latent, None),
            P("y", None, latent),
            P("y", latent),
            P("y", None, latent),
            P("y", None, latent, None),
            P(),
            P("y", latent, None),
        ),
        out_specs=(
            P("y", None, latent),
            P("y", latent),
            P("y", None, latent, None),
            P("y", None),
        ),
        check_vma=False,
    )
```

```python
import jax
import jax.numpy as jnp
from jax import lax
from jax.experimental import pallas as pl
from jax.experimental.pallas import tpu as pltpu
from jax.sharding import Mesh
from jax.sharding import PartitionSpec as P

SWAP = [(0, 1), (1, 0)]
BF16 = jnp.bfloat16
F32 = jnp.float32
VMEM = pl.BlockSpec(memory_space=pltpu.VMEM)
SMEM = pl.BlockSpec(memory_space=pltpu.SMEM)
ANY = pl.BlockSpec(memory_space=pl.ANY)
OVER_ROWS = (((0,), (0,)), ((), ()))


def params(mebibytes):
    return pltpu.CompilerParams(vmem_limit_bytes=mebibytes * 1024 * 1024)


def cost(flops, moved):
    return pl.CostEstimate(flops=flops, bytes_accessed=moved, transcendentals=0)


def swap_halves(block):
    middle = block.shape[0] // 2
    return jnp.concatenate([block[middle:], block[:middle]], axis=0)


def start_all(source, held, sems):
    copies = [pltpu.make_async_copy(source.at[i], held.at[i], sems.at[i]) for i in range(held.shape[0])]
    for copy in copies:
        copy.start()
    return copies


def copies_kernel(source, out, acts, sem):
    load = pltpu.make_async_copy(source, acts, sem)
    load.start()
    load.wait()
    tiles = [acts[0, :, start : start + 128].astype(F32) for start in range(0, acts.shape[2], 128)]
    packed = jnp.concatenate(tiles, axis=0).astype(BF16)
    out[...] = jnp.broadcast_to(packed[None], out.shape)


def copies_of_rows(acts, chips):
    _, held, width = acts.shape
    return pl.pallas_call(
        copies_kernel,
        in_specs=[ANY],
        out_specs=VMEM,
        scratch_shapes=[pltpu.VMEM(acts.shape, BF16), pltpu.SemaphoreType.DMA],
        out_shape=jax.ShapeDtypeStruct((chips, held * width // 128, 128), BF16),
        compiler_params=params(4),
        cost_estimate=cost(0, 2 * chips * held * width),
        name="copies_of_rows",
    )(acts)


def half_of(source, side, held):
    half = held.shape[2]
    return source.at[:, :, pl.ds(pl.multiple_of(side * half, half), half)]


def recon_kernel(layer, feats, feats_other, mine, got, placed, out):
    both = jnp.concatenate([feats[...], swap_halves(feats_other[...])], axis=1)
    for target in range(out.shape[0]):

        @pl.when(target < layer[0])
        def _():
            out[target] = jnp.zeros(out.shape[1:], BF16)

        @pl.when(target >= layer[0])
        def _():
            decoders = jnp.concatenate([mine[target], got[target]], axis=0)
            total = jnp.dot(both, decoders, preferred_element_type=F32)
            out[target] = total.astype(BF16)

            @pl.when(target == layer[0])
            def _():
                out[target] = (total - placed[...].astype(F32)).astype(BF16)


def recon_partials(layer, feats, feats_other, mine, got, placed):
    layers, latents, half = got.shape
    rows = feats.shape[0]
    return pl.pallas_call(
        recon_kernel,
        in_specs=[SMEM, VMEM, VMEM, VMEM, VMEM, VMEM],
        out_specs=VMEM,
        out_shape=jax.ShapeDtypeStruct((layers, rows, half), BF16),
        compiler_params=params(10),
        cost_estimate=cost(4 * layers * rows * latents * half, 6 * layers * rows * half),
        name="recon_partials",
    )(layer, feats, feats_other, mine, got, placed)


def add_kernel(pieces, out):
    total = jnp.sum(pieces[...].astype(F32), axis=0)
    quarter = out.shape[2]
    for group in range(total.shape[0] // 8):
        for side in range(2):
            tile = total[8 * group : 8 * group + 8, side * quarter : (side + 1) * quarter]
            out[2 * group + side] = tile.astype(BF16)


def add_pieces(pieces):
    count, rows, half = pieces.shape
    quarter = half // 2
    return pl.pallas_call(
        add_kernel,
        grid=(rows // 16,),
        in_specs=[pl.BlockSpec((count, 16, half), lambda step: (0, step, 0))],
        out_specs=pl.BlockSpec((4, 8, quarter), lambda step: (step, 0, 0)),
        out_shape=jax.ShapeDtypeStruct((rows // 4, 8, quarter), BF16),
        compiler_params=params(8),
        cost_estimate=cost(count * rows * half, 2 * count * rows * half),
        name="add_pieces",
    )(pieces)


def half_of_targets(layer, side, feats, err_of, decoder_of, grads, held, sems, total, sums):
    layers, latents, half = held.shape
    quarter = half // 2
    rows = feats.shape[0]
    lanes = pl.ds(pl.multiple_of(side * half, half), half)
    leaving = [pltpu.make_async_copy(held.at[t], grads.at[t, :, lanes], sems.at[t]) for t in range(layers)]

    def tile(target, part):
        return err_of(target)[:, part].reshape(rows, quarter)

    total[...] = jnp.zeros_like(total)
    for target in range(layers):
        decoder_of(target, wait=True)

        @pl.when(target < layer)
        def _():
            held[target] = jnp.zeros(held.shape[1:], BF16)

        @pl.when(target >= layer)
        def _():
            block = jnp.concatenate([tile(target, part) for part in range(2)], axis=1)
            held[target] = lax.dot_general(feats, block, OVER_ROWS, preferred_element_type=F32).astype(BF16)
            total[...] += lax.dot_general(
                block, decoder_of(target)[...], (((1,), (1,)), ((), ())), preferred_element_type=F32
            )

        leaving[target].start()

        @pl.when(target == layer)
        def _():
            for part in range(2):
                sums[:, part * quarter : (part + 1) * quarter] = jnp.sum(
                    tile(target, part).astype(F32), axis=0, keepdims=True
                )

    return leaving


def own_half_kernel(places, feats, errs, decoder, grads, back, sums, decoder_held, held, decoder_sems, sems):
    loads = start_all(half_of(decoder, places[1], decoder_held), decoder_held, decoder_sems)

    def decoder_of(target, wait=False):
        if wait:
            loads[target].wait()
        return decoder_held.at[target]

    def err_of(target, wait=False):
        return errs.at[target]

    leaving = half_of_targets(places[0], places[1], feats[...], err_of, decoder_of, grads, held, sems, back, sums)
    for copy in leaving:
        copy.wait()


def own_half(places, feats, errs, decoder):
    layers, latents, width = decoder.shape
    half = width // 2
    rows = feats.shape[0]
    block = pltpu.VMEM((layers, latents, half), BF16)
    sems = pltpu.SemaphoreType.DMA((layers,))
    return pl.pallas_call(
        own_half_kernel,
        in_specs=[SMEM, VMEM, VMEM, ANY],
        out_specs=[ANY, VMEM, VMEM],
        out_shape=[
            jax.ShapeDtypeStruct((layers, latents, 2 * half), BF16),
            jax.ShapeDtypeStruct((rows, latents), F32),
            jax.ShapeDtypeStruct((1, half), F32),
        ],
        scratch_shapes=[block, block, sems, sems],
        compiler_params=params(14),
        cost_estimate=cost(4 * layers * rows * latents * half, 6 * layers * latents * half),
        name="own_half",
    )(places, feats, errs, decoder)


def other_half_kernel(
    places, feats, gate, back, own_sums, errs, decoder, same, apart, grads_in,
    grads, sums, grad_enc, enc_sums,
    decoder_held, held, enc_held, total, other_sums, decoder_sems, sems, enc_sems,
):
    loads = start_all(half_of(decoder, 1 - places[1], decoder_held), decoder_held, decoder_sems)

    def err_of(target, wait=False):
        return errs.at[target]

    def decoder_of(target, wait=False):
        if wait:
            loads[target].wait()
        return decoder_held.at[target]

    leaving = half_of_targets(
        places[0], 1 - places[1], swap_halves(feats[...]), err_of, decoder_of, grads, held, sems, total, other_sums
    )
    dpre = ((back[...] + swap_halves(total[...])) * gate[...].astype(F32)).astype(BF16)
    enc_sums[...] = jnp.sum(dpre.astype(F32), axis=0, keepdims=True)
    parts, block, _ = enc_held.shape
    middle = same.shape[0]
    for part in range(parts):
        lanes = slice(part * block, (part + 1) * block)
        enc_held[part] = (
            lax.dot_general(same[:, lanes], dpre[:middle], OVER_ROWS, preferred_element_type=F32)
            + lax.dot_general(apart[:, lanes], dpre[middle:], OVER_ROWS, preferred_element_type=F32)
        ).astype(BF16)
        copy = pltpu.make_async_copy(enc_held.at[part], grad_enc.at[pl.ds(part * block, block)], enc_sems.at[part])
        copy.start()
        leaving.append(copy)
    half = own_sums.shape[1]

    @pl.when(places[1] == 0)
    def _():
        sums[:, :half] = own_sums[...]
        sums[:, half:] = other_sums[...]

    @pl.when(places[1] == 1)
    def _():
        sums[:, :half] = other_sums[...]
        sums[:, half:] = own_sums[...]

    for copy in leaving:
        copy.wait()


def other_half(places, feats, gate, back, own_sums, errs, decoder, same, apart, grads):
    layers, latents, width = decoder.shape
    rows, half = feats.shape[0], width // 2
    block = pltpu.VMEM((layers, latents, half), BF16)
    sems = pltpu.SemaphoreType.DMA((layers,))
    return pl.pallas_call(
        other_half_kernel,
        in_specs=[SMEM, VMEM, VMEM, VMEM, VMEM, VMEM, ANY, VMEM, VMEM, ANY],
        out_specs=[ANY, VMEM, ANY, VMEM],
        out_shape=[
            jax.ShapeDtypeStruct(grads.shape, BF16),
            jax.ShapeDtypeStruct((1, width), F32),
            jax.ShapeDtypeStruct((width, latents), BF16),
            jax.ShapeDtypeStruct((1, latents), F32),
        ],
        scratch_shapes=[
            block,
            block,
            pltpu.VMEM((4, width // 4, latents), BF16),
            pltpu.VMEM((rows, latents), F32),
            pltpu.VMEM((1, half), F32),
            sems,
            sems,
            sems,
        ],
        input_output_aliases={9: 0},
        compiler_params=params(20),
        cost_estimate=cost(6 * layers * rows * latents * half, 8 * layers * latents * half),
        name="other_half",
    )(places, feats, gate, back, own_sums, errs, decoder, same, apart, grads)


def per_device(acts, enc_weight, enc_bias, active, dec_weight, dec_bias, targets):
    layer, core = lax.axis_index("y"), lax.axis_index("c")
    chip, place = lax.axis_index(("x", "z")), lax.axis_index("z")
    decoder = dec_weight[0]
    layers, latents, width = decoder.shape
    half, quarter = width // 2, width // 4
    rows = active.shape[1]
    held = acts.shape[1]
    chips = rows // (2 * held)
    scale = rows ** (-0.5)

    tiles = width // 128
    copies = copies_of_rows(acts, chips)
    same = lax.all_to_all(copies, ("x", "z"), 0, 0, tiled=True)
    same = same.reshape(chips, tiles, held, 128).transpose(0, 2, 1, 3).reshape(chips * held, width)

    give = lax.dynamic_slice_in_dim(decoder, (1 - core) * half, half, axis=2)
    mine = lax.dynamic_slice_in_dim(decoder, core * half, half, axis=2)
    got = lax.ppermute(give, "c", SWAP)
    target_mine = lax.dynamic_slice_in_dim(targets[0], core * half, half, axis=1)
    target_give = lax.dynamic_slice_in_dim(targets[0], (1 - core) * half, half, axis=1)
    target_got = lax.ppermute(target_give, "c", SWAP)
    placed = jnp.zeros((rows, half), BF16)
    placed = lax.dynamic_update_slice_in_dim(placed, target_mine, chip * held, 0)
    placed = lax.dynamic_update_slice_in_dim(placed, target_got, rows // 2 + chip * held, 0)
    by_core = active[0].reshape(chips, 2, held, latents)
    active_rows = jnp.concatenate(
        [
            lax.dynamic_index_in_dim(by_core, which, 1, keepdims=False).reshape(rows // 2, latents)
            for which in (core, 1 - core)
        ],
        axis=0,
    )

    bias = lax.dynamic_slice(dec_bias, (layer, core * half + (place % 2) * quarter), (1, quarter))[0]
    same, mine, bias, active_rows = lax.optimization_barrier((same, mine, bias, active_rows))
    apart = lax.ppermute(same, "c", SWAP)
    pre = jnp.concatenate(
        [jnp.dot(part, enc_weight[0], preferred_element_type=F32) for part in (same, apart)], axis=0
    )
    feats = ((pre + enc_bias[0][None, :]) * active_rows.astype(F32)).astype(BF16)
    feats_other = lax.ppermute(feats, "c", SWAP)

    places = jnp.stack([layer, core]).astype(jnp.int32)
    partials = recon_partials(places, feats, feats_other, mine, got, placed)
    pieces = lax.all_to_all(partials.reshape(16, rows // 4, half), ("y", "x"), 0, 0, tiled=True)
    chunks = lax.all_to_all(add_pieces(pieces), "z", 0, 0, tiled=True)
    summed = jnp.sum(chunks.astype(F32), axis=0)
    err = ((summed + bias) * scale).astype(BF16)
    near = lax.all_to_all(jnp.broadcast_to(err[None], chunks.shape), "z", 0, 0, tiled=True)
    far = lax.all_to_all(jnp.broadcast_to(near[None], (16,) + near.shape), ("y", "x"), 0, 0, tiled=True)
    errs = far.reshape(layers, rows // 8, 2, 8, quarter)
    errs_other = lax.ppermute(errs, "c", SWAP)

    grads, back, own_sums = own_half(places, feats, errs, decoder)
    grads, sums, grad_enc, grad_enc_bias = other_half(
        places, feats, active_rows, back, own_sums, errs_other, decoder, same, apart, grads
    )
    return grad_enc[None], grad_enc_bias, grads[None], sums


def solution(mesh):
    split = Mesh(mesh.devices.reshape(4, 4, 8, 2), ("y", "x", "z", "c"))
    latent = ("x", "z", "c")
    return jax.shard_map(
        per_device,
        mesh=split,
        in_specs=(
            P("y", latent, None),
            P("y", None, latent),
            P("y", latent),
            P("y", None, latent),
            P("y", None, latent, None),
            P(),
            P("y", latent, None),
        ),
        out_specs=(
            P("y", None, latent),
            P("y", latent),
            P("y", None, latent, None),
            P("y", None),
        ),
        check_vma=False,
    )
```
